32 devices in a mesh: frame: 4 (over x, core), req: 8 (over z, y).
Axes of the slice: x: 2, y: 2, z: 4, core: 2. Of those that a mesh axis runs over, the one named last changes fastest.
Arguments:
- queries: bfloat16 [2, 4, 2048, 4096], P(None, 'frame', 'req'), may hold values from -160 to 160
- key_vectors: bfloat16 [2, 4, 2048, 4096], P(None, 'frame', 'req'), may hold values from -6 to 6
- value_vectors: bfloat16 [2, 4, 2048, 4096], P(None, 'frame', 'req'), may hold values from -6 to 6
- head_class: int32 [2, 32], replicated, may hold values from 0 to 1, as said below
Outputs:
- attended: bfloat16 [2, 4, 2048, 4096], P(None, 'frame', 'req')
The draws below stay inside these ranges and needn't reach their ends.
Inputs may be any that keep to these rules, and one draw needn't show every extreme that they name: `head_class`: exactly 32 entries are 1, the others 0.
All inputs are finite; a program needn't handle non-finite values.
Results may differ from the reference program's by a relative error of at most 0.003.
Values may be sent and summed in bfloat16 or wider, within the bound.
A program may use at most 320 MiB of HBM per device.

```python
import jax
import jax.numpy as jnp
from jax import lax

H = 32
HD = 128
TOKF = 2048
REQS = 2
FRAMES = 4
SPATIAL = 32


def key_field(key):
    shape = (REQS, FRAMES, TOKF, H * HD)
    base = jnp.clip(jax.random.normal(jax.random.fold_in(key, 7), shape, jnp.float32), -6.0, 6.0)
    field = base
    return field


def draw_queries(key, part):
    own_key = jax.random.fold_in(key, 11)
    result = jnp.clip(jax.random.normal(own_key, (REQS, FRAMES, TOKF, H * HD), jnp.float32), -6.0, 6.0)
    return result.astype(jnp.bfloat16)


def draw_key_vectors(key, part):
    field = key_field(key)
    return field.astype(jnp.bfloat16)


def draw_head_class(key, part):
    key = jax.random.fold_in(key, 23)
    weight_key, order_key = jax.random.split(key)
    head_weight = jax.random.randint(weight_key, (H,), 0, 4, dtype=jnp.int32)
    shuffled = jax.random.permutation(order_key, REQS * H).astype(jnp.int32)
    scores = head_weight[None, :] * (REQS * H) + shuffled.reshape(REQS, H)
    ranking = jnp.argsort(-scores.reshape(-1), stable=True).astype(jnp.int32)
    labels = jnp.zeros((REQS * H,), jnp.int32).at[ranking[:SPATIAL]].set(1)
    return labels.reshape(REQS, H)


def block_levels(key, dims, pieces, low, top_value):
    factor_of, own = 1.0, jax.random.fold_in(key, 6)
    for axis_at, blocks in pieces:
        draws = jnp.exp(jax.random.uniform(jax.random.fold_in(own, axis_at), (blocks,), jnp.float32, low / len(pieces), top_value / len(pieces)))
        factor_of = factor_of * jnp.repeat(draws, dims[axis_at] // blocks).reshape([-1 if axis == axis_at else 1 for axis in range(len(dims))])
    return factor_of


def gaussian(rng, extent, spread, most, cuts=(), kind=jnp.bfloat16):
    loudness = block_levels(rng, extent, cuts, -0.22, 0.18) if cuts else 1.0
    values = jax.random.normal(rng, extent, jnp.float32) * spread * loudness
    return jnp.minimum(jnp.maximum(values, -most), most).astype(kind)


def setup_inputs(seed: int = 0) -> dict:
    key_of = jax.random.split(jax.random.key(seed), 5)
    return {
        "queries": draw_queries(jax.random.fold_in(key_of[4], 71), 0),
        "key_vectors": draw_key_vectors(jax.random.fold_in(key_of[4], 71), 0),
        "value_vectors": gaussian(key_of[2], (REQS, FRAMES, TOKF, H * HD), 1.0, 6.0, ((1, 4), (2, 8))),
        "head_class": draw_head_class(jax.random.fold_in(key_of[4], 71), 0),
    }


def softmax_parts(scores):
    largest = jnp.max(scores, axis=-1, keepdims=True)
    exp_terms = jnp.exp(scores - largest)
    row_total = jnp.sum(exp_terms, axis=-1, keepdims=True)
    weights = lax.optimization_barrier(exp_terms.astype(jnp.bfloat16))
    return weights.astype(jnp.float32), row_total


def reference(queries, key_vectors, value_vectors, head_class):
    requests, frames, tokens, columns = queries.shape
    q_all = queries.reshape(requests, frames, tokens, H, HD)
    k_all = key_vectors.reshape(requests, frames, tokens, H, HD)
    v_all = value_vectors.reshape(requests, frames, tokens, H, HD)
    ranking = jnp.argsort(1 - head_class.reshape(-1), stable=True).astype(jnp.int32)
    spatial_ids = ranking[:SPATIAL]
    temporal_ids = ranking[SPATIAL:]
    scale = HD ** -0.5

    def one_frame(trio):
        q_rows, k_rows, v_rows = trio
        scores = jnp.einsum("qd,kd->qk", q_rows.astype(jnp.float32), k_rows.astype(jnp.float32)) * scale
        weights, row_total = softmax_parts(scores)
        mixed_rows = jnp.einsum("qk,kd->qd", weights, v_rows.astype(jnp.float32)) / row_total
        return mixed_rows.astype(jnp.bfloat16)

    def one_pair(index):
        request_idx = index // H
        head_idx = index % H
        trio = (q_all[request_idx, :, :, head_idx, :], k_all[request_idx, :, :, head_idx, :], v_all[request_idx, :, :, head_idx, :])
        return lax.map(one_frame, trio)

    spatial_out = lax.map(one_pair, spatial_ids)
    temp_req = temporal_ids // H
    temp_head = temporal_ids % H
    q_temp = q_all[temp_req, :, :, temp_head, :].astype(jnp.float32)
    k_temp = k_all[temp_req, :, :, temp_head, :].astype(jnp.float32)
    v_temp = v_all[temp_req, :, :, temp_head, :].astype(jnp.float32)
    scores = jnp.einsum("nftd,ngtd->nftg", q_temp, k_temp) * scale
    weights, row_total = softmax_parts(scores)
    temporal_out = (jnp.einsum("nftg,ngtd->nftd", weights, v_temp) / row_total).astype(jnp.bfloat16)
    merged = jnp.concatenate([spatial_out, temporal_out], axis=0)
    result = jnp.zeros((requests, frames, tokens, H, HD), jnp.bfloat16)
    result = result.at[ranking // H, :, :, ranking % H, :].set(merged)
    return result.reshape(requests, frames, tokens, columns)
```

```python
import functools

import jax
import jax.numpy as jnp
from jax import lax
from jax.experimental import pallas as pl
from jax.experimental.pallas import tpu as pltpu
from jax.sharding import PartitionSpec as P

SPATIAL = 32
MESH = pl.DeviceIdType.MESH
LOG2E = 1.4426950408889634


def attend(q, k, v, scale, mask=None):
    scores = lax.dot_general(q, k, (((1,), (1,)), ((), ())), preferred_element_type=jnp.float32)
    if mask is not None:
        scores = jnp.where(mask, scores, -jnp.inf)
    largest = jnp.max(scores, axis=-1, keepdims=True)
    terms = jnp.exp2((scores - largest) * (scale * LOG2E))
    total = jnp.sum(terms, axis=-1, keepdims=True)
    mixed = jnp.dot(terms.astype(jnp.bfloat16), v, preferred_element_type=jnp.float32)
    return (mixed / total).astype(jnp.bfloat16)


def kernel(
    frames, reqs, rounds, order, slots, q_hbm, k_hbm, v_hbm, out_hbm,
    src, sp_send, sp_recv, tm_send, tm_recv, so_send, to_send, out_recv,
    load_sem, store_sem, sp_ss, sp_rs, tm_ss, tm_rs, so_ss, so_rs, to_ss, to_rs,
):
    requests, _, rows, columns = q_hbm.shape
    hd = out_recv.shape[-1]
    heads = columns // hd
    pairs = requests * heads
    spatial = rounds * reqs
    chunk = (pairs - spatial) // rounds
    part = rows // frames
    scale = hd ** (-0.5)
    my_f, my_r = lax.axis_index("frame"), lax.axis_index("req")

    def head_at(ref, i):
        column = pl.multiple_of((i % heads) * hd, hd)
        return ref.at[i // heads, 0, :, pl.ds(column, hd)]

    def load_pair(i, _):
        for j, ref in enumerate((q_hbm, k_hbm, v_hbm)):
            pltpu.make_async_copy(head_at(ref, i), src.at[j, i], load_sem.at[j]).start()
        return 0

    lax.fori_loop(0, pairs, load_pair, 0)

    barrier = pltpu.get_barrier_semaphore()
    for step in range(1, reqs):
        pl.semaphore_signal(
            barrier, inc=1, device_id=(my_f, lax.rem(my_r + step, reqs)), device_id_type=MESH
        )
    for step in range(1, frames):
        pl.semaphore_signal(
            barrier, inc=1, device_id=(lax.rem(my_f + step, frames), my_r), device_id_type=MESH
        )
    pl.semaphore_wait(barrier, reqs + frames - 2)
    for j in range(3):
        pltpu.make_async_copy(src.at[j], src.at[j], load_sem.at[j]).wait()

    def source(j, slot):
        return src[j, order[slot]]

    def sp_copy(p, step):
        return pltpu.make_async_remote_copy(
            src_ref=sp_send.at[p, step],
            dst_ref=sp_recv.at[p, :, pl.ds(my_r * rows, rows), :],
            send_sem=sp_ss.at[p, step],
            recv_sem=sp_rs.at[p, step],
            device_id=(my_f, lax.rem(my_r + step, reqs)),
            device_id_type=MESH,
        )

    def tm_copy(c, step):
        dest = lax.rem(my_f + step, frames)
        return pltpu.make_async_remote_copy(
            src_ref=tm_send.at[dest, pl.ds(c * chunk, chunk)],
            dst_ref=tm_recv.at[my_f, pl.ds(c * chunk, chunk)],
            send_sem=tm_ss.at[c, step],
            recv_sem=tm_rs.at[c, step],
            device_id=(dest, my_r),
            device_id_type=MESH,
        )

    def so_copy(p, step):
        return pltpu.make_async_remote_copy(
            src_ref=so_send.at[p, step],
            dst_ref=out_recv.at[my_r * rounds + p],
            send_sem=so_ss.at[p, step],
            recv_sem=so_rs.at[p, step],
            device_id=(my_f, lax.rem(my_r + step, reqs)),
            device_id_type=MESH,
        )

    def to_copy(c, step):
        dest = lax.rem(my_f + step, frames)
        return pltpu.make_async_remote_copy(
            src_ref=to_send.at[dest, pl.ds(c * chunk, chunk)],
            dst_ref=out_recv.at[pl.ds(spatial + c * chunk, chunk), pl.ds(my_f * part, part), :],
            send_sem=to_ss.at[c, step],
            recv_sem=to_rs.at[c, step],
            device_id=(dest, my_r),
            device_id_type=MESH,
        )

    def send_round(p, _):
        def pack_spatial(step, _):
            slot = lax.rem(my_r + step, reqs) * rounds + p
            for j in range(3):
                sp_send[p, step, j] = source(j, slot)
            sp_copy(p, step).start()
            return 0

        lax.fori_loop(1, reqs, pack_spatial, 0)
        for j in range(3):
            sp_recv[p, j, pl.ds(my_r * rows, rows), :] = source(j, my_r * rounds + p)

        def pack_temporal(i, _):
            n = p * chunk + i
            for j in range(3):
                tm_send[:, n, j] = source(j, spatial + n).reshape(frames, part, hd)
                tm_recv[my_f, n, j] = tm_send[my_f, n, j]
            return 0

        lax.fori_loop(0, chunk, pack_temporal, 0)
        for step in range(1, frames):
            tm_copy(p, step).start()
        return 0

    lax.fori_loop(0, rounds, send_round, 0)

    side = frames * part
    position = lax.broadcasted_iota(jnp.int32, (side, side), 0) % part
    other = lax.broadcasted_iota(jnp.int32, (side, side), 1) % part

    def compute_round(p, _):
        for step in range(1, frames):
            tm_copy(p, step).wait_recv()

        def temporal_pair(i, _):
            n = p * chunk + i
            q, k, v = (tm_recv[:, n, j].reshape(side, hd) for j in range(3))
            mixed = attend(q, k, v, scale, position == other)
            to_send[:, n] = mixed.reshape(frames, part, hd)
            out_recv[spatial + n, pl.ds(my_f * part, part), :] = to_send[my_f, n]
            return 0

        lax.fori_loop(0, chunk, temporal_pair, 0)
        for step in range(1, frames):
            to_copy(p, step).start()

        def arrived(step, _):
            sp_copy(p, step).wait_recv()
            return 0

        lax.fori_loop(1, reqs, arrived, 0)

        def spatial_block(q_at):
            q = sp_recv[p, 0, pl.ds(q_at * rows, rows), :]
            return attend(q, sp_recv[p, 1], sp_recv[p, 2], scale)

        def spatial_step(step, _):
            so_send[p, step] = spatial_block(lax.rem(my_r + step, reqs))
            so_copy(p, step).start()
            return 0

        lax.fori_loop(1, reqs, spatial_step, 0)
        out_recv[my_r * rounds + p] = spatial_block(my_r)
        return 0

    lax.fori_loop(0, rounds, compute_round, 0)

    def finish_round(p, _):
        for step in range(1, frames):
            to_copy(p, step).wait_recv()
            to_copy(p, step).wait_send()
            tm_copy(p, step).wait_send()

        def finish_step(step, _):
            so_copy(p, step).wait_recv()
            so_copy(p, step).wait_send()
            sp_copy(p, step).wait_send()
            return 0

        lax.fori_loop(1, reqs, finish_step, 0)
        return 0

    lax.fori_loop(0, rounds, finish_round, 0)

    def place(i, _):
        src[0, i] = out_recv[slots[i]]
        pltpu.make_async_copy(src.at[0, i], head_at(out_hbm, i), store_sem).start()
        return 0

    lax.fori_loop(0, pairs, place, 0)
    pltpu.make_async_copy(src.at[0], src.at[0], store_sem).wait()


def per_device(frames, reqs, queries, key_vectors, value_vectors, head_class):
    requests, _, rows, columns = queries.shape
    heads = head_class.shape[1]
    hd = columns // heads
    pairs = requests * heads
    rounds = SPATIAL // reqs
    temporal = pairs - SPATIAL
    part = rows // frames
    inside = head_class.reshape(-1)
    index = jnp.arange(pairs, dtype=jnp.int32)
    count = jnp.sum(jnp.where(index[None, :] <= index[:, None], inside[None, :], 0), axis=1)
    slots = jnp.where(inside == 1, count - 1, SPATIAL + index - count).astype(jnp.int32)
    order = jnp.sum(
        jnp.where(slots[None, :] == index[:, None], index[None, :], 0), axis=1
    ).astype(jnp.int32)

    bf16 = jnp.bfloat16
    dma = pltpu.SemaphoreType.DMA
    return pl.pallas_call(
        functools.partial(kernel, frames, reqs, rounds),
        out_shape=jax.ShapeDtypeStruct(queries.shape, bf16),
        in_specs=[pl.BlockSpec(memory_space=pltpu.SMEM)] * 2
        + [pl.BlockSpec(memory_space=pl.ANY)] * 3,
        out_specs=pl.BlockSpec(memory_space=pl.ANY),
        scratch_shapes=[
            pltpu.VMEM((3, pairs, rows, hd), bf16),
            pltpu.VMEM((rounds, reqs, 3, rows, hd), bf16),
            pltpu.VMEM((rounds, 3, reqs * rows, hd), bf16),
            pltpu.VMEM((frames, temporal, 3, part, hd), bf16),
            pltpu.VMEM((frames, temporal, 3, part, hd), bf16),
            pltpu.VMEM((rounds, reqs, rows, hd), bf16),
            pltpu.VMEM((frames, temporal, part, hd), bf16),
            pltpu.VMEM((pairs, rows, hd), bf16),
            dma((3,)),
            dma,
            dma((rounds, reqs)),
            dma((rounds, reqs)),
            dma((rounds, frames)),
            dma((rounds, frames)),
            dma((rounds, reqs)),
            dma((rounds, reqs)),
            dma((rounds, frames)),
            dma((rounds, frames)),
        ],
        compiler_params=pltpu.CompilerParams(
            collective_id=0, has_side_effects=True, vmem_limit_bytes=60 * 1024 * 1024
        ),
        cost_estimate=pl.CostEstimate(
            flops=4 * rounds * (reqs * rows) ** 2 * hd,
            bytes_accessed=4 * queries.size * 2,
            transcendentals=rounds * (reqs * rows) ** 2,
        ),
    )(order, slots, queries, key_vectors, value_vectors)


def solution(mesh):
    return jax.shard_map(
        functools.partial(per_device, mesh.shape["frame"], mesh.shape["req"]),
        mesh=mesh,
        in_specs=(
            P(None, "frame", "req", None),
            P(None, "frame", "req", None),
            P(None, "frame", "req", None),
            P(),
        ),
        out_specs=P(None, "frame", "req", None),
        check_vma=False,
    )
```

```python
import functools

import jax
import jax.numpy as jnp
from jax import lax
from jax.experimental import pallas as pl
from jax.experimental.pallas import tpu as pltpu
from jax.sharding import PartitionSpec as P

SPATIAL = 32
MESH = pl.DeviceIdType.MESH
LOG2E = 1.4426950408889634


def attend(q, k, v, scale, mask=None):
    scores = lax.dot_general(q, k, (((1,), (1,)), ((), ())), preferred_element_type=jnp.float32)
    if mask is not None:
        scores = jnp.where(mask, scores, -jnp.inf)
    largest = jnp.max(scores, axis=-1, keepdims=True)
    terms = jnp.exp2((scores - largest) * (scale * LOG2E))
    total = jnp.sum(terms, axis=-1, keepdims=True)
    mixed = jnp.dot(terms.astype(jnp.bfloat16), v, preferred_element_type=jnp.float32)
    return (mixed / total).astype(jnp.bfloat16)


def head_at(ref, i, heads, hd):
    column = pl.multiple_of((i % heads) * hd, hd)
    return ref.at[i // heads, 0, :, pl.ds(column, hd)]


def kernel(
    frames, reqs, rounds, head_class, q_hbm, k_hbm, v_hbm, out_hbm,
    q_src, k_src, v_src, sp_send, sp_recv, tm_send, tm_recv, so_send, to_send,
    load_sem, sp_ss, sp_rs, tm_ss, tm_rs, so_ss, so_rs, to_ss, to_rs, own_so, own_to, counts,
):
    src = (q_src, k_src, v_src)
    requests, _, rows, columns = q_hbm.shape
    hd = out_hbm.shape[-1]
    heads = columns // hd
    pairs = requests * heads
    spatial = rounds * reqs
    chunk = (pairs - spatial) // rounds
    part = rows // frames
    scale = hd ** (-0.5)
    my_f, my_r = lax.axis_index("frame"), lax.axis_index("req")

    barrier = pltpu.get_barrier_semaphore()
    for step in range(1, reqs):
        pl.semaphore_signal(
            barrier, inc=1, device_id=(my_f, lax.rem(my_r + step, reqs)), device_id_type=MESH
        )
    for step in range(1, frames):
        pl.semaphore_signal(
            barrier, inc=1, device_id=(lax.rem(my_f + step, frames), my_r), device_id_type=MESH
        )
    def start_load(j, ref):
        def load_pair(i, _):
            pltpu.make_async_copy(
                head_at(ref, i, heads, hd), src[j].at[i], load_sem.at[j]
            ).start()
            return 0

        lax.fori_loop(0, pairs, load_pair, 0)

    start_load(0, q_hbm)

    def count_pair(i, count):
        count = count + head_class[i // heads, i % heads]
        counts[0, i] = count
        counts[1, i] = i + 1 - count
        return count

    lax.fori_loop(0, pairs, count_pair, jnp.int32(0))
    pl.semaphore_wait(barrier, reqs + frames - 2)

    def pair_of(kind, rank):
        pair = jnp.int32(0)
        width = pairs
        while width > 1:
            width = (width + 1) // 2
            probe = jnp.minimum(pair + width, pairs) - 1
            pair = jnp.where(counts[kind, probe] <= rank, probe + 1, pair)
        return jnp.minimum(pair, pairs - 1)

    def sp_copy(p, j, step):
        return pltpu.make_async_remote_copy(
            src_ref=sp_send.at[p, step, j],
            dst_ref=sp_recv.at[p, j, pl.ds(my_r * rows, rows), :],
            send_sem=sp_ss.at[p, j, step],
            recv_sem=sp_rs.at[p, j, step],
            device_id=(my_f, lax.rem(my_r + step, reqs)),
            device_id_type=MESH,
        )

    def tm_copy(c, step):
        dest = lax.rem(my_f + step, frames)
        return pltpu.make_async_remote_copy(
            src_ref=tm_send.at[dest, pl.ds(c * chunk, chunk)],
            dst_ref=tm_recv.at[my_f, pl.ds(c * chunk, chunk)],
            send_sem=tm_ss.at[c, step],
            recv_sem=tm_rs.at[c, step],
            device_id=(dest, my_r),
            device_id_type=MESH,
        )

    def so_copy(p, step):
        return pltpu.make_async_remote_copy(
            src_ref=so_send.at[p, step],
            dst_ref=out_hbm.at[my_r * rounds + p],
            send_sem=so_ss.at[p, step],
            recv_sem=so_rs.at[p, step],
            device_id=(my_f, lax.rem(my_r + step, reqs)),
            device_id_type=MESH,
        )

    def to_copy(c, step):
        dest = lax.rem(my_f + step, frames)
        return pltpu.make_async_remote_copy(
            src_ref=to_send.at[dest, pl.ds(c * chunk, chunk)],
            dst_ref=out_hbm.at[pl.ds(spatial + c * chunk, chunk), pl.ds(my_f * part, part), :],
            send_sem=to_ss.at[c, step],
            recv_sem=to_rs.at[c, step],
            device_id=(dest, my_r),
            device_id_type=MESH,
        )

    def own_so_copy(p):
        return pltpu.make_async_copy(
            so_send.at[p, 0], out_hbm.at[my_r * rounds + p], own_so.at[p]
        )

    def own_to_copy(c):
        return pltpu.make_async_copy(
            to_send.at[my_f, pl.ds(c * chunk, chunk)],
            out_hbm.at[pl.ds(spatial + c * chunk, chunk), pl.ds(my_f * part, part), :],
            own_to.at[c],
        )

    def send_spatial(p, j):
        def pack_spatial(step, _):
            sp_send[p, step, j] = src[j][pair_of(0, lax.rem(my_r + step, reqs) * rounds + p)]
            sp_copy(p, j, step).start()
            return 0

        lax.fori_loop(1, reqs, pack_spatial, 0)
        sp_recv[p, j, pl.ds(my_r * rows, rows), :] = src[j][pair_of(0, my_r * rounds + p)]

    def send_temporal(p):
        def pack_temporal(i, _):
            n = p * chunk + i
            pair = pair_of(1, n)
            for j in range(3):
                tm_send[:, n, j] = src[j][pair].reshape(frames, part, hd)
                tm_recv[my_f, n, j] = tm_send[my_f, n, j]
            return 0

        lax.fori_loop(0, chunk, pack_temporal, 0)
        for step in range(1, frames):
            tm_copy(p, step).start()

    for j in range(3):
        pltpu.make_async_copy(src[j], src[j], load_sem.at[j]).wait()
        send_spatial(0, j)
        if j == 0:
            start_load(1, k_hbm)
            start_load(2, v_hbm)
    send_temporal(0)

    def send_round(p, _):
        for j in range(3):
            send_spatial(p, j)
        send_temporal(p)
        return 0

    lax.fori_loop(1, rounds, send_round, 0)

    side = frames * part
    position = lax.broadcasted_iota(jnp.int32, (side, side), 0) % part
    other = lax.broadcasted_iota(jnp.int32, (side, side), 1) % part

    def compute_round(p, _):
        for step in range(1, frames):
            tm_copy(p, step).wait_recv()

        def temporal_pair(i, _):
            n = p * chunk + i
            q, k, v = (tm_recv[:, n, j].reshape(side, hd) for j in range(3))
            mixed = attend(q, k, v, scale, position == other)
            to_send[:, n] = mixed.reshape(frames, part, hd)
            return 0

        lax.fori_loop(0, chunk, temporal_pair, 0)
        for step in range(1, frames):
            to_copy(p, step).start()
        own_to_copy(p).start()

        def arrived(step, _):
            for j in range(3):
                sp_copy(p, j, step).wait_recv()
            return 0

        lax.fori_loop(1, reqs, arrived, 0)

        def spatial_block(q_at):
            q = sp_recv[p, 0, pl.ds(q_at * rows, rows), :]
            return attend(q, sp_recv[p, 1], sp_recv[p, 2], scale)

        def spatial_step(step, _):
            so_send[p, step] = spatial_block(lax.rem(my_r + step, reqs))
            so_copy(p, step).start()
            return 0

        lax.fori_loop(1, reqs, spatial_step, 0)
        so_send[p, 0] = spatial_block(my_r)
        own_so_copy(p).start()
        return 0

    lax.fori_loop(0, rounds, compute_round, 0)

    def finish_round(p, _):
        for step in range(1, frames):
            to_copy(p, step).wait_recv()
            to_copy(p, step).wait_send()
            tm_copy(p, step).wait_send()
        own_to_copy(p).wait()
        own_so_copy(p).wait()

        def finish_step(step, _):
            so_copy(p, step).wait_recv()
            so_copy(p, step).wait_send()
            for j in range(3):
                sp_copy(p, j, step).wait_send()
            return 0

        lax.fori_loop(1, reqs, finish_step, 0)
        return 0

    lax.fori_loop(0, rounds, finish_round, 0)


def arrange(head_class, packed, out_hbm, held, order, load_sem, store_sem):
    pairs, rows, hd = packed.shape
    heads = out_hbm.shape[3] // hd
    groups = load_sem.shape[0]
    group = pairs // groups
    loads = [
        pltpu.make_async_copy(
            packed.at[pl.ds(g * group, group)], held.at[pl.ds(g * group, group)], load_sem.at[g]
        )
        for g in range(groups)
    ]
    for load in loads:
        load.start()

    def place(i, count):
        inside = head_class[i // heads, i % heads]
        order[jnp.where(inside == 1, count, SPATIAL + i - count)] = i
        return count + inside

    lax.fori_loop(0, pairs, place, jnp.int32(0))
    for g in range(groups):
        loads[g].wait()

        def store(s, _):
            pltpu.make_async_copy(
                held.at[s], head_at(out_hbm, order[s], heads, hd), store_sem
            ).start()
            return 0

        lax.fori_loop(g * group, (g + 1) * group, store, 0)
    pltpu.make_async_copy(held, held, store_sem).wait()


def per_device(frames, reqs, queries, key_vectors, value_vectors, head_class):
    requests, _, rows, columns = queries.shape
    heads = head_class.shape[1]
    hd = columns // heads
    pairs = requests * heads
    rounds = SPATIAL // reqs
    temporal = pairs - SPATIAL
    part = rows // frames
    bf16 = jnp.bfloat16
    dma = pltpu.SemaphoreType.DMA
    packed = pl.pallas_call(
        functools.partial(kernel, frames, reqs, rounds),
        out_shape=jax.ShapeDtypeStruct((pairs, rows, hd), bf16),
        in_specs=[pl.BlockSpec(memory_space=pltpu.SMEM)]
        + [pl.BlockSpec(memory_space=pl.ANY)] * 3,
        out_specs=pl.BlockSpec(memory_space=pl.ANY),
        scratch_shapes=[
            pltpu.VMEM((pairs, rows, hd), bf16),
            pltpu.VMEM((pairs, rows, hd), bf16),
            pltpu.VMEM((pairs, rows, hd), bf16),
            pltpu.VMEM((rounds, reqs, 3, rows, hd), bf16),
            pltpu.VMEM((rounds, 3, reqs * rows, hd), bf16),
            pltpu.VMEM((frames, temporal, 3, part, hd), bf16),
            pltpu.VMEM((frames, temporal, 3, part, hd), bf16),
            pltpu.VMEM((rounds, reqs, rows, hd), bf16),
            pltpu.VMEM((frames, temporal, part, hd), bf16),
            dma((3,)),
            dma((rounds, 3, reqs)),
            dma((rounds, 3, reqs)),
            dma((rounds, frames)),
            dma((rounds, frames)),
            dma((rounds, reqs)),
            dma((rounds, reqs)),
            dma((rounds, frames)),
            dma((rounds, frames)),
            dma((rounds,)),
            dma((rounds,)),
            pltpu.SMEM((2, pairs), jnp.int32),
        ],
        compiler_params=pltpu.CompilerParams(
            collective_id=0, has_side_effects=True, vmem_limit_bytes=60 * 1024 * 1024
        ),
        cost_estimate=pl.CostEstimate(
            flops=4 * rounds * (reqs * rows) ** 2 * hd,
            bytes_accessed=4 * queries.size * 2,
            transcendentals=rounds * (reqs * rows) ** 2,
        ),
    )(head_class, queries, key_vectors, value_vectors)
    return pl.pallas_call(
        arrange,
        out_shape=jax.ShapeDtypeStruct(queries.shape, bf16),
        in_specs=[pl.BlockSpec(memory_space=pltpu.SMEM), pl.BlockSpec(memory_space=pl.ANY)],
        out_specs=pl.BlockSpec(memory_space=pl.ANY),
        scratch_shapes=[
            pltpu.VMEM((pairs, rows, hd), bf16),
            pltpu.SMEM((pairs,), jnp.int32),
            dma((4,)),
            dma,
        ],
        compiler_params=pltpu.CompilerParams(vmem_limit_bytes=60 * 1024 * 1024),
        cost_estimate=pl.CostEstimate(
            flops=0, bytes_accessed=queries.size * 4, transcendentals=0
        ),
    )(head_class, packed)


def solution(mesh):
    return jax.shard_map(
        functools.partial(per_device, mesh.shape["frame"], mesh.shape["req"]),
        mesh=mesh,
        in_specs=(
            P(None, "frame", "req", None),
            P(None, "frame", "req", None),
            P(None, "frame", "req", None),
            P(),
        ),
        out_specs=P(None, "frame", "req", None),
        check_vma=False,
    )
```

```python
import functools

import jax
import jax.numpy as jnp
from jax import lax
from jax.experimental import pallas as pl
from jax.experimental.pallas import tpu as pltpu
from jax.sharding import PartitionSpec as P

SPATIAL = 32
MESH = pl.DeviceIdType.MESH
LOG2E = 1.4426950408889634


def attend(q, k, v, scale, mask=None):
    scores = lax.dot_general(q, k, (((1,), (1,)), ((), ())), preferred_element_type=jnp.float32)
    if mask is not None:
        scores = jnp.where(mask, scores, -jnp.inf)
    largest = jnp.max(scores, axis=-1, keepdims=True)
    terms = jnp.exp2((scores - largest) * (scale * LOG2E))
    total = jnp.sum(terms, axis=-1, keepdims=True)
    mixed = jnp.dot(terms.astype(jnp.bfloat16), v, preferred_element_type=jnp.float32)
    return (mixed / total).astype(jnp.bfloat16)


def head_at(ref, i, heads, hd):
    column = pl.multiple_of((i % heads) * hd, hd)
    return ref.at[i // heads, 0, :, pl.ds(column, hd)]


def kernel(
    frames, reqs, rounds, head_class, q_hbm, k_hbm, v_hbm, out_hbm,
    q_src, k_src, v_src, sp_send, sp_recv, tm_send, tm_recv, so_send, to_send,
    load_sem, sp_ss, sp_rs, tm_ss, tm_rs, so_ss, so_rs, to_ss, to_rs, own_so, own_to, counts,
):
    src = (q_src, k_src, v_src)
    requests, _, rows, columns = q_hbm.shape
    hd = out_hbm.shape[-1]
    heads = columns // hd
    pairs = requests * heads
    spatial = rounds * reqs
    chunk = (pairs - spatial) // rounds
    part = rows // frames
    scale = hd ** (-0.5)
    my_f, my_r = lax.axis_index("frame"), lax.axis_index("req")

    barrier = pltpu.get_barrier_semaphore()
    for step in range(1, reqs):
        pl.semaphore_signal(
            barrier, inc=1, device_id=(my_f, lax.rem(my_r + step, reqs)), device_id_type=MESH
        )
    for step in range(1, frames):
        pl.semaphore_signal(
            barrier, inc=1, device_id=(lax.rem(my_f + step, frames), my_r), device_id_type=MESH
        )
    def start_load(j, ref):
        def load_pair(i, _):
            pltpu.make_async_copy(
                head_at(ref, i, heads, hd), src[j].at[i], load_sem.at[j]
            ).start()
            return 0

        lax.fori_loop(0, pairs, load_pair, 0)

    start_load(0, q_hbm)

    def count_pair(i, count):
        count = count + head_class[i // heads, i % heads]
        counts[0, i] = count
        counts[1, i] = i + 1 - count
        return count

    lax.fori_loop(0, pairs, count_pair, jnp.int32(0))
    pl.semaphore_wait(barrier, reqs + frames - 2)

    def pair_of(kind, rank):
        pair = jnp.int32(0)
        width = pairs
        while width > 1:
            width = (width + 1) // 2
            probe = jnp.minimum(pair + width, pairs) - 1
            pair = jnp.where(counts[kind, probe] <= rank, probe + 1, pair)
        return jnp.minimum(pair, pairs - 1)

    def sp_copy(p, j, step):
        return pltpu.make_async_remote_copy(
            src_ref=sp_send.at[p, step, j],
            dst_ref=sp_recv.at[p, j, pl.ds(my_r * rows, rows), :],
            send_sem=sp_ss.at[p, j, step],
            recv_sem=sp_rs.at[p, j, step],
            device_id=(my_f, lax.rem(my_r + step, reqs)),
            device_id_type=MESH,
        )

    def tm_copy(c, step):
        dest = lax.rem(my_f + step, frames)
        return pltpu.make_async_remote_copy(
            src_ref=tm_send.at[dest, pl.ds(c * chunk, chunk)],
            dst_ref=tm_recv.at[my_f, pl.ds(c * chunk, chunk)],
            send_sem=tm_ss.at[c, step],
            recv_sem=tm_rs.at[c, step],
            device_id=(dest, my_r),
            device_id_type=MESH,
        )

    def so_copy(p, step):
        return pltpu.make_async_remote_copy(
            src_ref=so_send.at[p, step],
            dst_ref=out_hbm.at[my_r * rounds + p],
            send_sem=so_ss.at[p, step],
            recv_sem=so_rs.at[p, step],
            device_id=(my_f, lax.rem(my_r + step, reqs)),
            device_id_type=MESH,
        )

    def to_copy(c, step):
        dest = lax.rem(my_f + step, frames)
        return pltpu.make_async_remote_copy(
            src_ref=to_send.at[dest, pl.ds(c * chunk, chunk)],
            dst_ref=out_hbm.at[pl.ds(spatial + c * chunk, chunk), pl.ds(my_f * part, part), :],
            send_sem=to_ss.at[c, step],
            recv_sem=to_rs.at[c, step],
            device_id=(dest, my_r),
            device_id_type=MESH,
        )

    def own_so_copy(p):
        return pltpu.make_async_copy(
            so_send.at[p, 0], out_hbm.at[my_r * rounds + p], own_so.at[p]
        )

    def own_to_copy(c):
        return pltpu.make_async_copy(
            to_send.at[my_f, pl.ds(c * chunk, chunk)],
            out_hbm.at[pl.ds(spatial + c * chunk, chunk), pl.ds(my_f * part, part), :],
            own_to.at[c],
        )

    def send_spatial(p, j):
        def pack_spatial(step, _):
            sp_send[p, step, j] = src[j][pair_of(0, lax.rem(my_r + step, reqs) * rounds + p)]
            sp_copy(p, j, step).start()
            return 0

        lax.fori_loop(1, reqs, pack_spatial, 0)
        sp_recv[p, j, pl.ds(my_r * rows, rows), :] = src[j][pair_of(0, my_r * rounds + p)]

    def send_temporal(p):
        def pack_temporal(i, _):
            n = p * chunk + i
            pair = pair_of(1, n)
            for j in range(3):
                tm_send[:, n, j] = src[j][pair].reshape(frames, part, hd)
                tm_recv[my_f, n, j] = tm_send[my_f, n, j]
            return 0

        lax.fori_loop(0, chunk, pack_temporal, 0)
        for step in range(1, frames):
            tm_copy(p, step).start()

    for j in range(3):
        pltpu.make_async_copy(src[j], src[j], load_sem.at[j]).wait()
        send_spatial(0, j)
        if j == 0:
            start_load(1, k_hbm)
            start_load(2, v_hbm)
    send_temporal(0)

    def send_round(p, _):
        for j in range(3):
            send_spatial(p, j)
        send_temporal(p)
        return 0

    lax.fori_loop(1, rounds, send_round, 0)

    side = frames * part
    position = lax.broadcasted_iota(jnp.int32, (side, side), 0) % part
    other = lax.broadcasted_iota(jnp.int32, (side, side), 1) % part

    def compute_round(p, _):
        for step in range(1, frames):
            tm_copy(p, step).wait_recv()

        def temporal_pair(i, _):
            n = p * chunk + i
            q, k, v = (tm_recv[:, n, j].reshape(side, hd) for j in range(3))
            mixed = attend(q, k, v, scale, position == other)
            to_send[:, n] = mixed.reshape(frames, part, hd)
            return 0

        lax.fori_loop(0, chunk, temporal_pair, 0)
        for step in range(1, frames):
            to_copy(p, step).start()
        own_to_copy(p).start()

        def arrived(step, _):
            for j in range(3):
                sp_copy(p, j, step).wait_recv()
            return 0

        lax.fori_loop(1, reqs, arrived, 0)

        def spatial_block(q_at):
            q = sp_recv[p, 0, pl.ds(q_at * rows, rows), :]
            return attend(q, sp_recv[p, 1], sp_recv[p, 2], scale)

        def spatial_step(step, _):
            so_send[p, step] = spatial_block(lax.rem(my_r + step, reqs))
            so_copy(p, step).start()
            return 0

        lax.fori_loop(1, reqs, spatial_step, 0)
        so_send[p, 0] = spatial_block(my_r)
        own_so_copy(p).start()
        return 0

    lax.fori_loop(0, rounds, compute_round, 0)

    def finish_round(p, _):
        for step in range(1, frames):
            to_copy(p, step).wait_recv()
            to_copy(p, step).wait_send()
            tm_copy(p, step).wait_send()
        own_to_copy(p).wait()
        own_so_copy(p).wait()

        def finish_step(step, _):
            so_copy(p, step).wait_recv()
            so_copy(p, step).wait_send()
            for j in range(3):
                sp_copy(p, j, step).wait_send()
            return 0

        lax.fori_loop(1, reqs, finish_step, 0)
        return 0

    lax.fori_loop(0, rounds, finish_round, 0)


def arrange(head_class, packed, out_hbm, held, order, load_sem, store_sem):
    pairs, rows, hd = packed.shape
    heads = out_hbm.shape[3] // hd
    groups = load_sem.shape[0]
    group = pairs // groups
    loads = [
        pltpu.make_async_copy(
            packed.at[pl.ds(g * group, group)], held.at[pl.ds(g * group, group)], load_sem.at[g]
        )
        for g in range(groups)
    ]
    for load in loads:
        load.start()

    def place(i, count):
        inside = head_class[i // heads, i % heads]
        order[jnp.where(inside == 1, count, SPATIAL + i - count)] = i
        return count + inside

    lax.fori_loop(0, pairs, place, jnp.int32(0))
    for g in range(groups):
        loads[g].wait()

        def store(s, _):
            pltpu.make_async_copy(
                held.at[s], head_at(out_hbm, order[s], heads, hd), store_sem
            ).start()
            return 0

        lax.fori_loop(g * group, (g + 1) * group, store, 0)
    pltpu.make_async_copy(held, held, store_sem).wait()


def per_device(frames, reqs, queries, key_vectors, value_vectors, head_class):
    requests, _, rows, columns = queries.shape
    heads = head_class.shape[1]
    hd = columns // heads
    pairs = requests * heads
    rounds = SPATIAL // reqs
    temporal = pairs - SPATIAL
    part = rows // frames
    bf16 = jnp.bfloat16
    dma = pltpu.SemaphoreType.DMA
    packed = pl.pallas_call(
        functools.partial(kernel, frames, reqs, rounds),
        out_shape=jax.ShapeDtypeStruct((pairs, rows, hd), bf16),
        in_specs=[pl.BlockSpec(memory_space=pltpu.SMEM)]
        + [pl.BlockSpec(memory_space=pl.ANY)] * 3,
        out_specs=pl.BlockSpec(memory_space=pl.ANY),
        scratch_shapes=[
            pltpu.VMEM((pairs, rows, hd), bf16),
            pltpu.VMEM((pairs, rows, hd), bf16),
            pltpu.VMEM((pairs, rows, hd), bf16),
            pltpu.VMEM((rounds, reqs, 3, rows, hd), bf16),
            pltpu.VMEM((rounds, 3, reqs * rows, hd), bf16),
            pltpu.VMEM((frames, temporal, 3, part, hd), bf16),
            pltpu.VMEM((frames, temporal, 3, part, hd), bf16),
            pltpu.VMEM((rounds, reqs, rows, hd), bf16),
            pltpu.VMEM((frames, temporal, part, hd), bf16),
            dma((3,)),
            dma((rounds, 3, reqs)),
            dma((rounds, 3, reqs)),
            dma((rounds, frames)),
            dma((rounds, frames)),
            dma((rounds, reqs)),
            dma((rounds, reqs)),
            dma((rounds, frames)),
            dma((rounds, frames)),
            dma((rounds,)),
            dma((rounds,)),
            pltpu.SMEM((2, pairs), jnp.int32),
        ],
        compiler_params=pltpu.CompilerParams(
            collective_id=0, has_side_effects=True, vmem_limit_bytes=60 * 1024 * 1024
        ),
        cost_estimate=pl.CostEstimate(
            flops=4 * rounds * (reqs * rows) ** 2 * hd,
            bytes_accessed=4 * queries.size * 2,
            transcendentals=rounds * (reqs * rows) ** 2,
        ),
    )(head_class, queries, key_vectors, value_vectors)
    return pl.pallas_call(
        arrange,
        out_shape=jax.ShapeDtypeStruct(queries.shape, bf16),
        in_specs=[pl.BlockSpec(memory_space=pltpu.SMEM), pl.BlockSpec(memory_space=pl.ANY)],
        out_specs=pl.BlockSpec(memory_space=pl.ANY),
        scratch_shapes=[
            pltpu.VMEM((pairs, rows, hd), bf16),
            pltpu.SMEM((pairs,), jnp.int32),
            dma((8,)),
            dma,
        ],
        compiler_params=pltpu.CompilerParams(vmem_limit_bytes=60 * 1024 * 1024),
        cost_estimate=pl.CostEstimate(
            flops=0, bytes_accessed=queries.size * 4, transcendentals=0
        ),
    )(head_class, packed)


def solution(mesh):
    return jax.shard_map(
        functools.partial(per_device, mesh.shape["frame"], mesh.shape["req"]),
        mesh=mesh,
        in_specs=(
            P(None, "frame", "req", None),
            P(None, "frame", "req", None),
            P(None, "frame", "req", None),
            P(),
        ),
        out_specs=P(None, "frame", "req", None),
        check_vma=False,
    )
```
